256 devices in a mesh: depth: 4 (over x_hi, core), rows: 64 (over y, x_lo, z).
Axes of the slice: x: 4 (x_hi: 2, x_lo: 2; x = x_hi * 2 + x_lo), y: 4, z: 8, core: 2. Of those that a mesh axis runs over, the one named last changes fastest.
Arguments:
- perturbation: float32 [8, 4096, 4096], P('depth', 'rows'), may hold values from -6 to 6
- level_set: float32 [8, 4096, 4096], P('depth', 'rows'), may hold values from -6 to 6
- labels: int32 [8, 4096, 4096], P('depth', 'rows'), may hold values from 0 to 3
- contrasts: float32 [4], replicated, may hold values from 0.8 to 4
- kernel: float32 [8, 4096, 4096], P('depth', 'rows'), may hold values from 0.3 to 1.5
Outputs:
- hessian_vector: float32 [8, 4096, 4096], P('depth', 'rows')
The draws below stay inside these ranges and needn't reach their ends.
All inputs are finite; a program needn't handle non-finite values.
Results may differ from the reference program's by a relative error of at most 0.0001.
Values sent between devices are 32-bit elements; how exact they have to be, the bound alone decides.
No kernel may reach another device: no remote copies, remote signals or barrier semaphores. Data moves between devices by JAX's collectives and lax.ppermute only.
A program may use at most 128 MiB of HBM per device.

```python
import math
import jax
import jax.numpy as jnp

N = 4096
UNITS = 4
LAYERS = 8


def place_ends(entries, rng, smallest, high):
    dims = entries.shape
    place = [jax.random.randint(jax.random.fold_in(rng, axis), (), 0, dims[axis]) for axis in range(len(dims))]
    entries = entries.at[tuple(place)].set(smallest)
    longest = dims.index(max(dims))
    place[longest] = (place[longest] + 1) % dims[longest]
    return entries.at[tuple(place)].set(high)


def block_scale(key, shape, split, least, high):
    gain = 1.0
    for position, parts in split:
        draws = jax.random.uniform(jax.random.fold_in(jax.random.fold_in(key, 6), position), (parts,), jnp.float32, least / len(split), high / len(split))
        gain = gain * jnp.repeat(jnp.exp(draws), shape[position] // parts).reshape((-1,) + (1,) * (len(shape) - 1 - position))
    return gain


def bell_draw(key, shape, deviation, most, split=(), dtype=jnp.bfloat16):
    factor_of = block_scale(key, shape, split, -0.22, 0.18) if split else 1.0
    entries = jax.random.normal(key, shape, jnp.float32) * deviation * factor_of
    return jnp.minimum(jnp.maximum(entries, -most), most).astype(dtype)


def setup_inputs(seed: int = 0) -> dict:
    keys = jax.random.split(jax.random.key(seed), 6)
    perturbation = bell_draw(keys[0], (LAYERS, N, N), 1.0, 6.0, ((0, 4), (1, 64)), jnp.float32)
    level_set = bell_draw(keys[1], (LAYERS, N, N), 1.0, 6.0, ((0, 4), (1, 64)), jnp.float32)
    labels = place_ends(jax.random.randint(keys[2], (LAYERS, N, N), 0, UNITS), jax.random.fold_in(keys[2], 1), 0, UNITS - 1).astype(jnp.int32)
    contrasts = jnp.clip(jnp.exp(jax.random.uniform(keys[3], (UNITS,), jnp.float32, math.log(0.8), math.log(4.0))), 0.8, 4.0)
    kernel = jnp.clip(0.3 + 1.2 * jax.random.uniform(keys[4], (LAYERS, N, N), jnp.float32) ** block_scale(keys[4], (LAYERS, N, N), ((0, 4), (1, 64)), -0.2, 0.2), 0.3, 1.5)
    return dict(perturbation=perturbation, level_set=level_set, labels=labels, contrasts=contrasts, kernel=kernel)


smoothing = 0.5

def unit_weight(labels, level_set, contrasts):
    chosen = jnp.zeros(labels.shape, jnp.float32)
    for unit in range(contrasts.shape[0]):
        chosen = jnp.where(labels == unit, contrasts[unit], chosen)
    delta = smoothing / (math.pi * (level_set * level_set + smoothing * smoothing))
    return chosen * delta

def hartley_last(field):
    spectral = jnp.fft.fft(field, axis=-1)
    return ((spectral.real - spectral.imag) / math.sqrt(N)).astype(jnp.float32)

def reference(perturbation, level_set, labels, contrasts, kernel):
    data_spectrum = jnp.zeros((N, N), jnp.float32)
    weights = []
    for layer in range(LAYERS):
        weight = unit_weight(labels[layer], level_set[layer], contrasts)
        weights.append(weight)
        masked = weight * perturbation[layer]
        turned = hartley_last(hartley_last(masked).T)
        data_spectrum = data_spectrum + kernel[layer] * turned
    outputs = []
    for layer in range(LAYERS):
        scaled = kernel[layer] * data_spectrum
        back = hartley_last(hartley_last(scaled).T)
        outputs.append(weights[layer] * back)
    return jnp.stack(outputs)
```

```python
import math

import jax
import jax.numpy as jnp
import ml_dtypes
import numpy as np
from jax import lax
from jax.experimental import pallas as pl
from jax.experimental.pallas import tpu as pltpu
from jax.sharding import PartitionSpec as P

smoothing = 0.5
length = 4096
chunks = 2
big = 60
bf16 = jnp.bfloat16


def cas(angle):
    return np.cos(angle) + np.sin(angle)


def stage_matrices(small, wide):
    b = np.arange(wide)[None, :]
    m = np.arange(wide)[:, None]
    turn = 2.0 * np.pi / wide
    low = np.concatenate([cas(turn * b * m), np.sin(turn * b * m) - np.cos(turn * b * m)], axis=1)
    high = np.concatenate(
        [cas(turn * b * (m + 1)), np.cos(turn * b * (m + 1)) - np.sin(turn * b * (m + 1))], axis=1
    )
    pair = np.concatenate([low, high], axis=0)
    first = np.zeros_like(pair)
    first[:wide, :wide] = cas(turn * b * m)
    full = 2.0 * np.pi / (small * wide)
    first[wide:, wide:] = cas(full * ((b * (small // 2 + small * m)) % (small * wide)))
    scale = 1.0 / math.sqrt(small * wide)
    return pair * scale, first * scale


def twiddles(small, wide):
    k = np.arange(small // 2)[:, None]
    b = np.arange(wide)[None, :]
    angle = 2.0 * np.pi / (small * wide) * k * b
    return np.stack([np.cos(angle), -np.sin(angle)], axis=1).astype(np.float32)


def split_matrix(matrix, axis):
    high = matrix.astype(ml_dtypes.bfloat16)
    low = (matrix - high.astype(np.float64)).astype(ml_dtypes.bfloat16)
    return np.concatenate([high, high, low], axis=axis)


def split_value(value, axis):
    high = value.astype(bf16)
    low = (value - high.astype(jnp.float32)).astype(bf16)
    return jnp.concatenate([high, low, high], axis=axis)


def dot(a, b, dims):
    return lax.dot_general(a, b, (dims, ((), ())), preferred_element_type=jnp.float32)


def real_fft(values):
    n = len(values)
    if n == 1:
        return [(values[0], None)]
    if n == 2:
        return [(values[0] + values[1], None), (values[0] - values[1], None)]
    even = real_fft(values[0::2])
    odd = real_fft(values[1::2])
    out = [None] * (n // 2 + 1)
    out[0] = (even[0][0] + odd[0][0], None)
    out[n // 2] = (even[0][0] - odd[0][0], None)
    out[n // 4] = (even[n // 4][0], -odd[n // 4][0])
    for k in range(1, n // 4):
        c, s = math.cos(2.0 * math.pi * k / n), math.sin(2.0 * math.pi * k / n)
        er, ei = even[k]
        orr, oi = odd[k]
        if 8 * k == n:
            tr, ti = (orr + oi) * c, (oi - orr) * c
        else:
            tr, ti = orr * c + oi * s, oi * c - orr * s
        out[k] = (er + tr, ei + ti)
        out[n // 2 - k] = (er - tr, ti - ei)
    return out


def real_fft_adjoint(spectrum):
    n = 2 * (len(spectrum) - 1)
    if n == 2:
        return [spectrum[0][0] + spectrum[1][0], spectrum[0][0] - spectrum[1][0]]
    even = [None] * (n // 4 + 1)
    odd = [None] * (n // 4 + 1)
    even[0] = (spectrum[0][0] + spectrum[n // 2][0], None)
    odd[0] = (spectrum[0][0] - spectrum[n // 2][0], None)
    even[n // 4] = (spectrum[n // 4][0], None)
    odd[n // 4] = (-spectrum[n // 4][1], None)
    for k in range(1, n // 4):
        c, s = math.cos(2.0 * math.pi * k / n), math.sin(2.0 * math.pi * k / n)
        ar, ai = spectrum[k]
        br, bi = spectrum[n // 2 - k]
        even[k] = (ar + br, ai - bi)
        dr, di = ar - br, ai + bi
        if 8 * k == n:
            odd[k] = ((dr - di) * c, (dr + di) * c)
        else:
            odd[k] = (dr * c - di * s, dr * s + di * c)
    out = [None] * n
    out[0::2] = real_fft_adjoint(even)
    out[1::2] = real_fft_adjoint(odd)
    return out


row_small, row_wide = 32, 128
col_small, col_wide = 64, 64
row_step = 32
steps = 128 // row_step


def row_forward(contrasts, labels, level_set, perturbation, turn, pair, first, weight, *rest):
    sends, parts = rest[:chunks], rest[chunks]
    step = pl.program_id(0)
    for tile in range(row_step // 8):
        rows = pl.ds(tile * 8, 8)
        fields = []
        for a in range(row_small):
            at = (rows, pl.ds(a * row_wide, row_wide))
            unit = labels[at]
            chosen = jnp.where(
                unit < 2,
                jnp.where(unit == 0, contrasts[0], contrasts[1]),
                jnp.where(unit == 2, contrasts[2], contrasts[3]),
            )
            level = level_set[at]
            here = chosen / (level * level + smoothing * smoothing)
            weight[at] = here
            fields.append(here * perturbation[at])
        spectrum = real_fft(fields)
        into = pl.ds(pl.multiple_of(step * row_step + tile * 8, 8), 8)
        parts[0, into, :row_wide] = spectrum[0][0]
        parts[0, into, row_wide:] = spectrum[row_small // 2][0]
        for k in range(1, row_small // 2):
            re, im = spectrum[k]
            c, s = turn[k, 0:1, :], turn[k, 1:2, :]
            parts[k, into, :row_wide] = re * c - im * s
            parts[k, into, row_wide:] = im * c + re * s

    @pl.when(step == steps - 1)
    def _():
        for k in range(row_small // 2):
            value = split_value(parts[k], 1)
            matrix = (pair if k else first)[...]
            out = dot(matrix, value, ((1,), (1,)))
            for half, place in enumerate((k, row_small - k if k else row_small // 2)):
                for chunk in range(chunks):
                    begin = (half * chunks + chunk) * 64
                    sends[chunk][pl.ds(place, 64, stride=row_small), :] = out[begin : begin + 64]


def row_backward(weight, received0, received1, turn, pair, first, out, parts):
    step = pl.program_id(0)
    received = (received0, received1)

    @pl.when(step == 0)
    def _():
        for k in range(row_small // 2):
            value = jnp.concatenate(
                [
                    received[chunk][pl.ds(place, 64, stride=row_small), :]
                    for place in (k, row_small - k if k else row_small // 2)
                    for chunk in range(chunks)
                ],
                axis=0,
            )
            value = split_value(value, 0)
            matrix = (pair if k else first)[...]
            parts[k] = dot(value, matrix, ((0,), (0,)))

    for tile in range(row_step // 8):
        rows = pl.ds(tile * 8, 8)
        source = pl.ds(pl.multiple_of(step * row_step + tile * 8, 8), 8)
        spectrum = [(parts[0, source, :row_wide], None)]
        for k in range(1, row_small // 2):
            tr, ti = parts[k, source, :row_wide], parts[k, source, row_wide:]
            c, s = turn[k, 0:1, :], turn[k, 1:2, :]
            spectrum.append((tr * c + ti * s, ti * c - tr * s))
        spectrum.append((parts[0, source, row_wide:], None))
        fields = real_fft_adjoint(spectrum)
        for a in range(row_small):
            at = (rows, pl.ds(a * row_wide, row_wide))
            out[at] = fields[a] * weight[at]


def column_forward(received, kernel, turn, pair, first, data, parts):
    spectrum = real_fft([received[r] for r in range(col_small)])
    parts[0, :, :128] = spectrum[0][0]
    parts[0, :, 128:] = spectrum[col_small // 2][0]
    for k in range(1, col_small // 2):
        re, im = spectrum[k]
        c, s = turn[k, 0:1, :], turn[k, 1:2, :]
        parts[k, :, :128] = re * c - im * s
        parts[k, :, 128:] = im * c + re * s
    half = col_small // 2
    value = split_value(parts[...].reshape(half * 8, 256), 1)
    rest = dot(value, pair[...], ((1,), (0,)))
    zero = dot(split_value(parts[0], 1), first[...], ((1,), (0,)))
    rest = rest.reshape(half, 8, 256)
    for k in range(half):
        spectra = (zero if k == 0 else rest[k]) * kernel[k]
        data[k] = spectra[:, :128] + spectra[:, 128:]


def column_backward(data, kernel, turn, pair, first, out, parts):
    half = col_small // 2
    both = jnp.concatenate([data[...], data[...]], axis=2)
    scaled = both * kernel[...]
    value = split_value(scaled.reshape(half * 8, 256), 1)
    parts[...] = dot(value, pair[...], ((1,), (0,))).reshape(half, 8, 256)
    parts[0] = dot(split_value(scaled[0], 1), first[...], ((1,), (0,)))
    spectrum = [(parts[0, :, :128], None)]
    for k in range(1, half):
        tr, ti = parts[k, :, :128], parts[k, :, 128:]
        c, s = turn[k, 0:1, :], turn[k, 1:2, :]
        spectrum.append((tr * c + ti * s, ti * c - tr * s))
    spectrum.append((parts[0, :, 128:], None))
    fields = real_fft_adjoint(spectrum)
    for r in range(col_small):
        out[r] = fields[r]


def whole(shape):
    return pl.BlockSpec(shape, lambda *_: (0,) * len(shape))


def params(mib):
    return pltpu.CompilerParams(vmem_limit_bytes=mib * 1024 * 1024)


def cost(flops, moved):
    return pl.CostEstimate(flops=flops, bytes_accessed=moved, transcendentals=0)


def column_matrices():
    out = []
    for matrix in stage_matrices(col_small, col_wide):
        both = np.zeros((2, 2, col_wide, 2, 2, col_wide))
        shaped = matrix.reshape(2, col_wide, 2, col_wide)
        for layer in range(2):
            both[layer, :, :, :, layer, :] = shaped
        out.append(both.reshape(256, 256))
    return out


def row_matrices():
    out = []
    for matrix in stage_matrices(row_small, row_wide):
        shaped = matrix.reshape(2, row_wide // chunks, chunks, 2 * row_wide)
        out.append(shaped.swapaxes(1, 2).reshape(256, 256))
    return out


def sum_over_depth(value):
    place = lax.axis_index("depth")
    core = place % 2
    swap_core = [(0, 1), (1, 0), (2, 3), (3, 2)]
    swap_chip = [(0, 2), (1, 3), (2, 0), (3, 1)]
    halves = value.reshape((2, value.shape[0] // 2) + value.shape[1:])
    mine = lax.dynamic_index_in_dim(halves, core, 0, keepdims=False)
    other = lax.dynamic_index_in_dim(halves, 1 - core, 0, keepdims=False)
    mine = mine + lax.ppermute(other, "depth", swap_core)
    mine = mine + lax.ppermute(mine, "depth", swap_chip)
    other = lax.ppermute(mine, "depth", swap_core)
    lower = jnp.where(core == 0, mine, other)
    upper = jnp.where(core == 0, other, mine)
    return jnp.concatenate([lower, upper], axis=0)


def kernel_in_pairs(kernel, *rest):
    outs, turned = rest[:chunks], rest[chunks]
    for tile in range(length // 128):
        lanes = pl.ds(tile * 128, 128)
        turned[lanes, :] = kernel[:, lanes].T
    for k in range(col_small // 2):
        places = (k, col_small - k if k else col_small // 2)
        pair = jnp.concatenate(
            [turned[pl.ds(place, col_wide, stride=col_small), :] for place in places], axis=0
        ).T
        for chunk in range(chunks):
            for layer in range(2):
                begin = layer * 64 + chunk * 32
                outs[chunk][k, :, layer * 128 : layer * 128 + 128] = pair[begin : begin + 32]


def on_device(perturbation, level_set, labels, contrasts, kernel):
    f32 = jnp.float32
    rows = [x.reshape(128, length) for x in (labels, level_set, perturbation)]
    scaled = contrasts * (smoothing / math.pi)
    row_turn = jnp.asarray(twiddles(row_small, row_wide))
    col_turn = twiddles(col_small, col_wide)
    col_turn = jnp.asarray(np.concatenate([col_turn, col_turn], axis=2))
    row_pair, row_first = row_matrices()
    col_pair, col_first = column_matrices()

    row_block = pl.BlockSpec((row_step, length), lambda i: (i, 0))
    sent = [(col_small * 32, 128)] * chunks
    weight, *sends = pl.pallas_call(
        row_forward,
        grid=(steps,),
        in_specs=[
            pl.BlockSpec(memory_space=pltpu.SMEM),
            row_block,
            row_block,
            row_block,
            whole((16, 2, 128)),
            whole((256, 768)),
            whole((256, 768)),
        ],
        out_specs=[row_block] + [whole(s) for s in sent],
        out_shape=[jax.ShapeDtypeStruct((128, length), f32)]
        + [jax.ShapeDtypeStruct(s, f32) for s in sent],
        scratch_shapes=[pltpu.VMEM((16, 128, 256), f32)],
        compiler_params=params(big),
        cost_estimate=cost(2 * 256 * 768 * 128 * 16, 12 * 2**20),
        name="row_forward",
    )(
        scaled,
        *rows,
        row_turn,
        jnp.asarray(split_matrix(row_pair, 1)),
        jnp.asarray(split_matrix(row_first, 1)),
    )

    kernels = pl.pallas_call(
        kernel_in_pairs,
        out_shape=[jax.ShapeDtypeStruct((32, 32, 256), f32)] * chunks,
        scratch_shapes=[pltpu.VMEM((length, 128), f32)],
        compiler_params=params(big),
        cost_estimate=cost(2 * 10**9, 4 * 2**20),
        name="kernel_in_pairs",
    )(kernel.reshape(128, length))

    tile = lambda n, lanes: pl.BlockSpec((n, 8, lanes), lambda i: (0, i, 0))
    mid = dict(grid=(4,), compiler_params=params(40))
    mid["cost_estimate"] = cost(2 * 768 * 256 * 1024, 5 * 2**19)
    mid["scratch_shapes"] = [pltpu.VMEM((32, 8, 256), f32)]
    constants = [whole((32, 2, 128)), whole((768, 256)), whole((768, 256))]
    forward = pl.pallas_call(
        column_forward,
        in_specs=[tile(64, 128), tile(32, 256)] + constants,
        out_specs=tile(32, 128),
        out_shape=jax.ShapeDtypeStruct((32, 32, 128), f32),
        name="column_forward",
        **mid,
    )
    backward = pl.pallas_call(
        column_backward,
        in_specs=[tile(32, 128), tile(32, 256)] + constants,
        out_specs=tile(64, 128),
        out_shape=jax.ShapeDtypeStruct((64, 32, 128), f32),
        name="column_backward",
        **mid,
    )
    forward_constants = [jnp.asarray(split_matrix(m.T, 0)) for m in (col_pair, col_first)]
    backward_constants = [jnp.asarray(split_matrix(m, 0)) for m in (col_pair, col_first)]

    returned = []
    for chunk in range(chunks):
        received = lax.all_to_all(
            sends[chunk].reshape(64, 32, 128), "rows", split_axis=0, concat_axis=0, tiled=True
        )
        local = forward(received, kernels[chunk], col_turn, *forward_constants)
        data = sum_over_depth(local)
        back = backward(data, kernels[chunk], col_turn, *backward_constants)
        back = lax.all_to_all(back, "rows", split_axis=0, concat_axis=0, tiled=True)
        returned.append(back.reshape(2048, 128))

    out = pl.pallas_call(
        row_backward,
        grid=(steps,),
        in_specs=[
            row_block,
            whole((2048, 128)),
            whole((2048, 128)),
            whole((16, 2, 128)),
            whole((768, 256)),
            whole((768, 256)),
        ],
        out_specs=row_block,
        out_shape=jax.ShapeDtypeStruct((128, length), f32),
        scratch_shapes=[pltpu.VMEM((16, 128, 256), f32)],
        compiler_params=params(big),
        cost_estimate=cost(2 * 256 * 768 * 128 * 16, 6 * 2**20),
        name="row_backward",
    )(
        weight,
        *returned,
        row_turn,
        jnp.asarray(split_matrix(row_pair, 0)),
        jnp.asarray(split_matrix(row_first, 0)),
    )
    return out.reshape(perturbation.shape)


def solution(mesh):
    in_specs = (
        P("depth", "rows", None),
        P("depth", "rows", None),
        P("depth", "rows", None),
        P(),
        P("depth", "rows", None),
    )
    out_specs = P("depth", "rows", None)
    return jax.shard_map(
        on_device, mesh=mesh, in_specs=in_specs, out_specs=out_specs, check_vma=False
    )
```

```python
import math

import jax
import jax.numpy as jnp
import ml_dtypes
import numpy as np
from jax import lax
from jax.experimental import pallas as pl
from jax.experimental.pallas import tpu as pltpu
from jax.sharding import PartitionSpec as P

smoothing = 0.5
length = 4096
big = 60
bf16 = jnp.bfloat16


def cas(angle):
    return np.cos(angle) + np.sin(angle)


def stage_matrices(small, wide):
    b = np.arange(wide)[None, :]
    m = np.arange(wide)[:, None]
    turn = 2.0 * np.pi / wide
    low = np.concatenate([cas(turn * b * m), np.sin(turn * b * m) - np.cos(turn * b * m)], axis=1)
    high = np.concatenate(
        [cas(turn * b * (m + 1)), np.cos(turn * b * (m + 1)) - np.sin(turn * b * (m + 1))], axis=1
    )
    pair = np.concatenate([low, high], axis=0)
    first = np.zeros_like(pair)
    first[:wide, :wide] = cas(turn * b * m)
    full = 2.0 * np.pi / (small * wide)
    first[wide:, wide:] = cas(full * ((b * (small // 2 + small * m)) % (small * wide)))
    scale = 1.0 / math.sqrt(small * wide)
    return pair * scale, first * scale


def twiddles(small, wide):
    k = np.arange(small // 2)[:, None]
    b = np.arange(wide)[None, :]
    angle = 2.0 * np.pi / (small * wide) * k * b
    return np.stack([np.cos(angle), -np.sin(angle)], axis=1).astype(np.float32)


def split_matrix(matrix, axis):
    high = matrix.astype(ml_dtypes.bfloat16)
    low = (matrix - high.astype(np.float64)).astype(ml_dtypes.bfloat16)
    return np.concatenate([high, high, low], axis=axis)


def split_value(value, axis):
    high = value.astype(bf16)
    low = (value - high.astype(jnp.float32)).astype(bf16)
    return jnp.concatenate([high, low, high], axis=axis)


def dot(a, b, dims):
    return lax.dot_general(a, b, (dims, ((), ())), preferred_element_type=jnp.float32)


def real_fft(values):
    n = len(values)
    if n == 1:
        return [(values[0], None)]
    if n == 2:
        return [(values[0] + values[1], None), (values[0] - values[1], None)]
    even = real_fft(values[0::2])
    odd = real_fft(values[1::2])
    out = [None] * (n // 2 + 1)
    out[0] = (even[0][0] + odd[0][0], None)
    out[n // 2] = (even[0][0] - odd[0][0], None)
    out[n // 4] = (even[n // 4][0], -odd[n // 4][0])
    for k in range(1, n // 4):
        c, s = math.cos(2.0 * math.pi * k / n), math.sin(2.0 * math.pi * k / n)
        er, ei = even[k]
        orr, oi = odd[k]
        if 8 * k == n:
            tr, ti = (orr + oi) * c, (oi - orr) * c
        else:
            tr, ti = orr * c + oi * s, oi * c - orr * s
        out[k] = (er + tr, ei + ti)
        out[n // 2 - k] = (er - tr, ti - ei)
    return out


def real_fft_adjoint(spectrum):
    n = 2 * (len(spectrum) - 1)
    if n == 2:
        return [spectrum[0][0] + spectrum[1][0], spectrum[0][0] - spectrum[1][0]]
    even = [None] * (n // 4 + 1)
    odd = [None] * (n // 4 + 1)
    even[0] = (spectrum[0][0] + spectrum[n // 2][0], None)
    odd[0] = (spectrum[0][0] - spectrum[n // 2][0], None)
    even[n // 4] = (spectrum[n // 4][0], None)
    odd[n // 4] = (-spectrum[n // 4][1], None)
    for k in range(1, n // 4):
        c, s = math.cos(2.0 * math.pi * k / n), math.sin(2.0 * math.pi * k / n)
        ar, ai = spectrum[k]
        br, bi = spectrum[n // 2 - k]
        even[k] = (ar + br, ai - bi)
        dr, di = ar - br, ai + bi
        if 8 * k == n:
            odd[k] = ((dr - di) * c, (dr + di) * c)
        else:
            odd[k] = (dr * c - di * s, dr * s + di * c)
    out = [None] * n
    out[0::2] = real_fft_adjoint(even)
    out[1::2] = real_fft_adjoint(odd)
    return out


row_small, row_wide = 32, 128
col_small, col_wide = 64, 64
row_step = 32
steps = 128 // row_step


def block_rows(k, odd):
    return pl.ds((2 * odd + k // 16) * 64 * 16 + k % 16, 64, stride=16)


def row_forward(contrasts, labels, level_set, perturbation, turn, pair, first, weight, send, parts):
    step = pl.program_id(0)
    scaled = [contrasts[unit] * (smoothing / math.pi) for unit in range(4)]
    for tile in range(row_step // 8):
        rows = pl.ds(tile * 8, 8)
        fields = []
        for a in range(row_small):
            at = (rows, pl.ds(a * row_wide, row_wide))
            unit = labels[at]
            chosen = jnp.where(
                unit < 2,
                jnp.where(unit == 0, scaled[0], scaled[1]),
                jnp.where(unit == 2, scaled[2], scaled[3]),
            )
            level = level_set[at]
            here = chosen / (level * level + smoothing * smoothing)
            weight[at] = here
            fields.append(here * perturbation[at])
        spectrum = real_fft(fields)
        into = pl.ds(pl.multiple_of(step * row_step + tile * 8, 8), 8)
        parts[0, into, :row_wide] = spectrum[0][0]
        parts[0, into, row_wide:] = spectrum[row_small // 2][0]
        for k in range(1, row_small // 2):
            re, im = spectrum[k]
            c, s = turn[k, 0:1, :], turn[k, 1:2, :]
            parts[k, into, :row_wide] = re * c - im * s
            parts[k, into, row_wide:] = im * c + re * s

    @pl.when(step == steps - 1)
    def _():
        for k in range(row_small // 2):
            value = split_value(parts[k], 1)
            matrix = (pair if k else first)[...]
            out = dot(matrix, value, ((1,), (1,)))
            for half, place in enumerate((k, row_small - k if k else row_small // 2)):
                for odd in range(2):
                    begin = (half * 2 + odd) * 64
                    send[block_rows(place, odd), :] = out[begin : begin + 64]


def row_backward(weight, received, turn, pair, first, out, parts):
    step = pl.program_id(0)

    @pl.when(step == 0)
    def _():
        for k in range(row_small // 2):
            value = jnp.concatenate(
                [
                    received[block_rows(place, odd), :]
                    for place in (k, row_small - k if k else row_small // 2)
                    for odd in range(2)
                ],
                axis=0,
            )
            value = split_value(value, 0)
            matrix = (pair if k else first)[...]
            parts[k] = dot(value, matrix, ((0,), (0,)))

    for tile in range(row_step // 8):
        rows = pl.ds(tile * 8, 8)
        source = pl.ds(pl.multiple_of(step * row_step + tile * 8, 8), 8)
        spectrum = [(parts[0, source, :row_wide], None)]
        for k in range(1, row_small // 2):
            tr, ti = parts[k, source, :row_wide], parts[k, source, row_wide:]
            c, s = turn[k, 0:1, :], turn[k, 1:2, :]
            spectrum.append((tr * c + ti * s, ti * c - tr * s))
        spectrum.append((parts[0, source, row_wide:], None))
        fields = real_fft_adjoint(spectrum)
        for a in range(row_small):
            at = (rows, pl.ds(a * row_wide, row_wide))
            out[at] = fields[a] * weight[at]


def column(place, received, kernel, turn, pair, first, pair_back, first_back, out, parts, data):
    half = col_small // 2
    for e in range(4):
        source = place[0] ^ e
        spectrum = real_fft([received[source, r] for r in range(col_small)])
        parts[e, 0, :, :128] = spectrum[0][0]
        parts[e, 0, :, 128:] = spectrum[half][0]
        for k in range(1, half):
            re, im = spectrum[k]
            c, s = turn[k, 0:1, :], turn[k, 1:2, :]
            parts[e, k, :, :128] = re * c - im * s
            parts[e, k, :, 128:] = im * c + re * s
        rest = dot(split_value(parts[e].reshape(half * 8, 256), 1), pair[...], ((1,), (0,)))
        zero = dot(split_value(parts[e, 0], 1), first[...], ((1,), (0,)))
        rest = rest.reshape(half, 8, 256)
        for k in range(half):
            spectra = (zero if k == 0 else rest[k]) * kernel[e, k]
            spectra = spectra[:, :128] + spectra[:, 128:]
            data[k] = spectra if e == 0 else data[k] + spectra
    for e in range(4):
        scaled = jnp.concatenate([data[...], data[...]], axis=2) * kernel[e]
        value = split_value(scaled.reshape(half * 8, 256), 1)
        parts[e] = dot(value, pair_back[...], ((1,), (0,))).reshape(half, 8, 256)
        parts[e, 0] = dot(split_value(scaled[0], 1), first_back[...], ((1,), (0,)))
        spectrum = [(parts[e, 0, :, :128], None)]
        for k in range(1, half):
            tr, ti = parts[e, k, :, :128], parts[e, k, :, 128:]
            c, s = turn[k, 0:1, :], turn[k, 1:2, :]
            spectrum.append((tr * c + ti * s, ti * c - tr * s))
        spectrum.append((parts[e, 0, :, 128:], None))
        fields = real_fft_adjoint(spectrum)
        for r in range(col_small):
            out[place[0] ^ e, r] = fields[r]


def whole(shape):
    return pl.BlockSpec(shape, lambda *_: (0,) * len(shape))


def params(mib):
    return pltpu.CompilerParams(vmem_limit_bytes=mib * 1024 * 1024)


def cost(flops, moved):
    return pl.CostEstimate(flops=flops, bytes_accessed=moved, transcendentals=0)


def column_matrices():
    out = []
    for matrix in stage_matrices(col_small, col_wide):
        both = np.zeros((2, 2, col_wide, 2, 2, col_wide))
        shaped = matrix.reshape(2, col_wide, 2, col_wide)
        for layer in range(2):
            both[layer, :, :, :, layer, :] = shaped
        out.append(both.reshape(256, 256))
    return out


def row_matrices():
    out = []
    for matrix in stage_matrices(row_small, row_wide):
        shaped = matrix.reshape(2, row_wide // 2, 2, 2 * row_wide)
        out.append(shaped.swapaxes(1, 2).reshape(256, 256))
    return out


def kernel_in_pairs(*refs):
    sources, out, turned = refs[:4], refs[4], refs[5]
    for tile in range(length // 128):
        lanes = pl.ds(tile * 128, 128)
        turned[lanes, :] = jnp.concatenate([x[:, lanes] for x in sources], axis=0).T
    for k in range(col_small // 2):
        places = (k, col_small - k if k else col_small // 2)
        pair = jnp.concatenate(
            [turned[pl.ds(place, col_wide, stride=col_small), :] for place in places], axis=0
        ).T
        for e in range(4):
            for layer in range(2):
                begin = e * 32 + layer * 16
                out[e, k, :, layer * 128 : layer * 128 + 128] = pair[begin : begin + 16]


def exchange_kernel(kernel):
    place = lax.axis_index("depth")
    out = []
    for e in range(4):
        block = lax.dynamic_slice_in_dim(kernel, (place ^ e) * 16, 16, axis=1)
        if e:
            block = lax.ppermute(block, "depth", [(d, d ^ e) for d in range(4)])
        out.append(block.reshape(32, length))
    return out


def on_device(perturbation, level_set, labels, contrasts, kernel):
    f32 = jnp.float32
    rows = [x.reshape(128, length) for x in (labels, level_set, perturbation)]
    row_turn = jnp.asarray(twiddles(row_small, row_wide))
    col_turn = twiddles(col_small, col_wide)
    col_turn = jnp.asarray(np.concatenate([col_turn, col_turn], axis=2))
    row_pair, row_first = row_matrices()
    col_pair, col_first = column_matrices()

    row_block = pl.BlockSpec((row_step, length), lambda i: (i, 0))
    weight, send = pl.pallas_call(
        row_forward,
        grid=(steps,),
        in_specs=[
            pl.BlockSpec(memory_space=pltpu.SMEM),
            row_block,
            row_block,
            row_block,
            whole((16, 2, 128)),
            whole((256, 768)),
            whole((256, 768)),
        ],
        out_specs=[row_block, whole((length, 128))],
        out_shape=[
            jax.ShapeDtypeStruct((128, length), f32),
            jax.ShapeDtypeStruct((length, 128), f32),
        ],
        scratch_shapes=[pltpu.VMEM((16, 128, 256), f32)],
        compiler_params=params(big),
        cost_estimate=cost(2 * 256 * 768 * 128 * 16, 12 * 2**20),
        name="row_forward",
    )(
        contrasts,
        *rows,
        row_turn,
        jnp.asarray(split_matrix(row_pair, 1)),
        jnp.asarray(split_matrix(row_first, 1)),
    )

    send, kernel = lax.optimization_barrier((send, kernel))
    received = lax.all_to_all(
        send.reshape(256, 16, 128), ("depth", "rows"), split_axis=0, concat_axis=0, tiled=True
    )
    kernels = pl.pallas_call(
        kernel_in_pairs,
        out_shape=jax.ShapeDtypeStruct((4, 32, 16, 256), f32),
        scratch_shapes=[pltpu.VMEM((length, 128), f32)],
        compiler_params=params(16),
        cost_estimate=cost(2 * 10**9, 4 * 2**20),
        name="kernel_in_pairs",
    )(*exchange_kernel(kernel))

    block = pl.BlockSpec((4, 64, 8, 128), lambda i: (0, 0, i, 0))
    back = pl.pallas_call(
        column,
        grid=(2,),
        in_specs=[
            pl.BlockSpec(memory_space=pltpu.SMEM),
            block,
            pl.BlockSpec((4, 32, 8, 256), lambda i: (0, 0, i, 0)),
            whole((32, 2, 128)),
        ]
        + [whole((768, 256))] * 4,
        out_specs=block,
        out_shape=jax.ShapeDtypeStruct((4, 64, 16, 128), f32),
        scratch_shapes=[pltpu.VMEM((4, 32, 8, 256), f32), pltpu.VMEM((32, 8, 128), f32)],
        compiler_params=params(32),
        cost_estimate=cost(2 * 768 * 256 * 4096, 6 * 2**20),
        name="column",
    )(
        lax.axis_index("depth").reshape(1),
        received.reshape(4, 64, 16, 128),
        kernels,
        col_turn,
        *[jnp.asarray(split_matrix(m.T, 0)) for m in (col_pair, col_first)],
        *[jnp.asarray(split_matrix(m, 0)) for m in (col_pair, col_first)],
    )
    returned = lax.all_to_all(
        back.reshape(256, 16, 128), ("depth", "rows"), split_axis=0, concat_axis=0, tiled=True
    )

    out = pl.pallas_call(
        row_backward,
        grid=(steps,),
        in_specs=[
            row_block,
            whole((length, 128)),
            whole((16, 2, 128)),
            whole((768, 256)),
            whole((768, 256)),
        ],
        out_specs=row_block,
        out_shape=jax.ShapeDtypeStruct((128, length), f32),
        scratch_shapes=[pltpu.VMEM((16, 128, 256), f32)],
        compiler_params=params(24),
        cost_estimate=cost(2 * 256 * 768 * 128 * 16, 6 * 2**20),
        name="row_backward",
    )(
        weight,
        returned.reshape(length, 128),
        row_turn,
        jnp.asarray(split_matrix(row_pair, 0)),
        jnp.asarray(split_matrix(row_first, 0)),
    )
    return out.reshape(perturbation.shape)


def solution(mesh):
    in_specs = (
        P("depth", "rows", None),
        P("depth", "rows", None),
        P("depth", "rows", None),
        P(),
        P("depth", "rows", None),
    )
    out_specs = P("depth", "rows", None)
    return jax.shard_map(
        on_device, mesh=mesh, in_specs=in_specs, out_specs=out_specs, check_vma=False
    )
```

```python
import math

import jax
import jax.numpy as jnp
import ml_dtypes
import numpy as np
from jax import lax
from jax.experimental import pallas as pl
from jax.experimental.pallas import tpu as pltpu
from jax.sharding import PartitionSpec as P

smoothing = 0.5
length = 4096
big = 60
bf16 = jnp.bfloat16


def cas(angle):
    return np.cos(angle) + np.sin(angle)


def stage_matrices(small, wide):
    b = np.arange(wide)[None, :]
    m = np.arange(wide)[:, None]
    turn = 2.0 * np.pi / wide
    low = np.concatenate([cas(turn * b * m), np.sin(turn * b * m) - np.cos(turn * b * m)], axis=1)
    high = np.concatenate(
        [cas(turn * b * (m + 1)), np.cos(turn * b * (m + 1)) - np.sin(turn * b * (m + 1))], axis=1
    )
    pair = np.concatenate([low, high], axis=0)
    first = np.zeros_like(pair)
    first[:wide, :wide] = cas(turn * b * m)
    full = 2.0 * np.pi / (small * wide)
    first[wide:, wide:] = cas(full * ((b * (small // 2 + small * m)) % (small * wide)))
    scale = 1.0 / math.sqrt(small * wide)
    return pair * scale, first * scale


def twiddles(small, wide):
    k = np.arange(small // 2 + 1)[:, None]
    b = np.arange(wide)[None, :]
    angle = 2.0 * np.pi / (small * wide) * k * b
    return np.stack([np.cos(angle), -np.sin(angle)], axis=1).astype(np.float32)


def split_matrix(matrix, axis):
    high = matrix.astype(ml_dtypes.bfloat16)
    low = (matrix - high.astype(np.float64)).astype(ml_dtypes.bfloat16)
    return np.concatenate([high, high, low], axis=axis)


def split_value(value, axis):
    high = value.astype(bf16)
    low = (value - high.astype(jnp.float32)).astype(bf16)
    return jnp.concatenate([high, low, high], axis=axis)


def dot(a, b, dims):
    return lax.dot_general(a, b, (dims, ((), ())), preferred_element_type=jnp.float32)


def real_fft(values):
    n = len(values)
    if n == 1:
        return [(values[0], None)]
    if n == 2:
        return [(values[0] + values[1], None), (values[0] - values[1], None)]
    even = real_fft(values[0::2])
    odd = real_fft(values[1::2])
    out = [None] * (n // 2 + 1)
    out[0] = (even[0][0] + odd[0][0], None)
    out[n // 2] = (even[0][0] - odd[0][0], None)
    out[n // 4] = (even[n // 4][0], -odd[n // 4][0])
    for k in range(1, n // 4):
        c, s = math.cos(2.0 * math.pi * k / n), math.sin(2.0 * math.pi * k / n)
        er, ei = even[k]
        orr, oi = odd[k]
        if 8 * k == n:
            tr, ti = (orr + oi) * c, (oi - orr) * c
        else:
            tr, ti = orr * c + oi * s, oi * c - orr * s
        out[k] = (er + tr, ei + ti)
        out[n // 2 - k] = (er - tr, ti - ei)
    return out


def real_fft_adjoint(spectrum):
    n = 2 * (len(spectrum) - 1)
    if n == 2:
        return [spectrum[0][0] + spectrum[1][0], spectrum[0][0] - spectrum[1][0]]
    even = [None] * (n // 4 + 1)
    odd = [None] * (n // 4 + 1)
    even[0] = (spectrum[0][0] + spectrum[n // 2][0], None)
    odd[0] = (spectrum[0][0] - spectrum[n // 2][0], None)
    even[n // 4] = (spectrum[n // 4][0], None)
    odd[n // 4] = (-spectrum[n // 4][1], None)
    for k in range(1, n // 4):
        c, s = math.cos(2.0 * math.pi * k / n), math.sin(2.0 * math.pi * k / n)
        ar, ai = spectrum[k]
        br, bi = spectrum[n // 2 - k]
        even[k] = (ar + br, ai - bi)
        dr, di = ar - br, ai + bi
        if 8 * k == n:
            odd[k] = ((dr - di) * c, (dr + di) * c)
        else:
            odd[k] = (dr * c - di * s, dr * s + di * c)
    out = [None] * n
    out[0::2] = real_fft_adjoint(even)
    out[1::2] = real_fft_adjoint(odd)
    return out


row_small, row_wide = 32, 128
col_small, col_wide = 64, 64
row_step = 32
steps = 128 // row_step


def block_rows(k, odd):
    return pl.ds((2 * odd + k // 16) * 64 * 16 + k % 16, 64, stride=16)


def row_forward(contrasts, labels, level_set, perturbation, turn, pair, first, send, *scratch):
    label_buf, level_buf, field_buf, turn_buf, pair_buf, first_buf, parts, block_sem, const_sem = scratch
    copies = []
    for step in range(steps):
        rows = pl.ds(step * row_step, row_step)
        for i, (source, into) in enumerate(
            ((labels, label_buf), (level_set, level_buf), (perturbation, field_buf))
        ):
            copies.append(pltpu.make_async_copy(source.at[rows], into.at[rows], block_sem.at[i, step]))
    constants = [
        pltpu.make_async_copy(source, into, const_sem.at[i])
        for i, (source, into) in enumerate(((turn, turn_buf), (pair, pair_buf), (first, first_buf)))
    ]
    constants[0].start()
    for copy in copies:
        copy.start()
    for copy in constants[1:]:
        copy.start()
    scaled = [contrasts[unit] * (smoothing / math.pi) for unit in range(4)]
    constants[0].wait()
    for step in range(steps):
        for copy in copies[3 * step : 3 * step + 3]:
            copy.wait()

        def tile_of(tile, carry):
            rows = pl.ds(pl.multiple_of(step * row_step + tile * 8, 8), 8)
            fields = []
            for a in range(row_small):
                at = (rows, pl.ds(a * row_wide, row_wide))
                fields.append(unit_weight(scaled, label_buf[at], level_buf[at]) * field_buf[at])
            spectrum = real_fft(fields)
            parts[0, rows, :row_wide] = spectrum[0][0]
            parts[0, rows, row_wide:] = spectrum[row_small // 2][0]
            for k in range(1, row_small // 2):
                re, im = spectrum[k]
                c, s = turn_buf[k, 0:1, :], turn_buf[k, 1:2, :]
                parts[k, rows, :row_wide] = re * c - im * s
                parts[k, rows, row_wide:] = im * c + re * s
            return carry

        lax.fori_loop(0, row_step // 8, tile_of, 0)
    for copy in constants[1:]:
        copy.wait()
    for k in range(row_small // 2):
        value = split_value(parts[k], 1)
        out = dot(value, (pair_buf if k else first_buf)[...], ((1,), (0,))).T
        for half, place in enumerate((k, row_small - k if k else row_small // 2)):
            for odd in range(2):
                begin = (half * 2 + odd) * 64
                send[block_rows(place, odd), :] = out[begin : begin + 64]


def unit_weight(scaled, unit, level):
    chosen = jnp.where(
        unit < 2,
        jnp.where(unit == 0, scaled[0], scaled[1]),
        jnp.where(unit == 2, scaled[2], scaled[3]),
    )
    return chosen / (level * level + smoothing * smoothing)


def row_backward(contrasts, labels, level_set, received, turn, pair, first, out, parts):
    step = pl.program_id(0)
    scaled = [contrasts[unit] * (smoothing / math.pi) for unit in range(4)]

    @pl.when(step == 0)
    def _():
        for k in range(row_small // 2):
            value = jnp.concatenate(
                [
                    received[block_rows(place, odd), :]
                    for place in (k, row_small - k if k else row_small // 2)
                    for odd in range(2)
                ],
                axis=0,
            )
            value = split_value(value, 0)
            matrix = (pair if k else first)[...]
            parts[k] = dot(value, matrix, ((0,), (0,)))

    for tile in range(row_step // 8):
        rows = pl.ds(tile * 8, 8)
        source = pl.ds(pl.multiple_of(step * row_step + tile * 8, 8), 8)
        spectrum = [(parts[0, source, :row_wide], None)]
        for k in range(1, row_small // 2):
            tr, ti = parts[k, source, :row_wide], parts[k, source, row_wide:]
            c, s = turn[k, 0:1, :], turn[k, 1:2, :]
            spectrum.append((tr * c + ti * s, ti * c - tr * s))
        spectrum.append((parts[0, source, row_wide:], None))
        fields = real_fft_adjoint(spectrum)
        for a in range(row_small):
            at = (rows, pl.ds(a * row_wide, row_wide))
            out[at] = fields[a] * unit_weight(scaled, labels[at], level_set[at])


def column(place, received, kernel, turn, matrix, matrix_back, out, parts, data):
    half = col_small // 2
    lanes = (slice(0, 64), slice(64, 128), slice(128, 192), slice(192, 256))
    blank = jnp.zeros((8, 64), jnp.float32)
    parts[:, half + 1] = jnp.zeros((4, 8, 256), jnp.float32)
    for e in range(4):
        source = place[0] ^ e
        spectrum = real_fft([received[source, r] for r in range(col_small)])
        parts[e, 0, :, :128] = spectrum[0][0]
        parts[e, 0, :, 128:] = jnp.zeros((8, 128), jnp.float32)
        parts[e, half, :, :128] = spectrum[half][0] * turn[half, 0:1, :]
        parts[e, half, :, 128:] = spectrum[half][0] * turn[half, 1:2, :]
        for k in range(1, half):
            re, im = spectrum[k]
            c, s = turn[k, 0:1, :], turn[k, 1:2, :]
            parts[e, k, :, :128] = re * c - im * s
            parts[e, k, :, 128:] = im * c + re * s
        value = split_value(parts[e].reshape(-1, 256), 1)
        result = dot(value, matrix[...], ((1,), (0,))).reshape(half + 2, 8, 256)
        zero, last = result[0], result[half]
        first = jnp.concatenate(
            [zero[:, lanes[0]], last[:, lanes[0]], zero[:, lanes[2]], last[:, lanes[2]]], axis=1
        )
        for k in range(half):
            spectra = (result[k] if k else first) * kernel[e, k]
            spectra = spectra[:, :128] + spectra[:, 128:]
            data[k] = spectra if e == 0 else data[k] + spectra
    for e in range(4):
        for k in range(half):
            scaled = jnp.concatenate([data[k], data[k]], axis=1) * kernel[e, k]
            if k:
                parts[e, k] = scaled
            else:
                low, high, low2, high2 = [scaled[:, at] for at in lanes]
                parts[e, 0] = jnp.concatenate([low, blank, low2, blank], axis=1)
                parts[e, half] = jnp.concatenate([high, blank, high2, blank], axis=1)
        value = split_value(parts[e].reshape(-1, 256), 1)
        parts[e] = dot(value, matrix_back[...], ((1,), (0,))).reshape(half + 2, 8, 256)
        spectrum = [(parts[e, 0, :, :128], None)]
        for k in range(1, half + 1):
            tr, ti = parts[e, k, :, :128], parts[e, k, :, 128:]
            c, s = turn[k, 0:1, :], turn[k, 1:2, :]
            spectrum.append((tr * c + ti * s, ti * c - tr * s if k < half else None))
        fields = real_fft_adjoint(spectrum)
        for r in range(col_small):
            out[place[0] ^ e, r] = fields[r]


def whole(shape):
    return pl.BlockSpec(shape, lambda *_: (0,) * len(shape))


def params(mib):
    return pltpu.CompilerParams(vmem_limit_bytes=mib * 1024 * 1024)


def cost(flops, moved):
    return pl.CostEstimate(flops=flops, bytes_accessed=moved, transcendentals=0)


def column_matrix():
    both = np.zeros((2, 2, col_wide, 2, 2, col_wide))
    shaped = stage_matrices(col_small, col_wide)[0].reshape(2, col_wide, 2, col_wide)
    for layer in range(2):
        both[layer, :, :, :, layer, :] = shaped
    return both.reshape(256, 256)


def row_matrices():
    out = []
    for matrix in stage_matrices(row_small, row_wide):
        shaped = matrix.reshape(2, row_wide // 2, 2, 2 * row_wide)
        out.append(shaped.swapaxes(1, 2).reshape(256, 256))
    return out


def kernel_in_pairs(*refs):
    sources, out, turned = refs[:4], refs[4], refs[5]
    for tile in range(length // 128):
        lanes = pl.ds(tile * 128, 128)
        turned[lanes, :] = jnp.concatenate([x[:, lanes] for x in sources], axis=0).T
    for k in range(col_small // 2):
        places = (k, col_small - k if k else col_small // 2)
        pair = jnp.concatenate(
            [turned[pl.ds(place, col_wide, stride=col_small), :] for place in places], axis=0
        ).T
        for e in range(4):
            for layer in range(2):
                begin = e * 32 + layer * 16
                out[e, k, :, layer * 128 : layer * 128 + 128] = pair[begin : begin + 16]


def exchange_kernel(kernel):
    place = lax.axis_index("depth")
    out = []
    for e in range(4):
        block = lax.dynamic_slice_in_dim(kernel, (place ^ e) * 16, 16, axis=1)
        if e:
            block = lax.ppermute(block, "depth", [(d, d ^ e) for d in range(4)])
        out.append(block.reshape(32, length))
    return out


def on_device(perturbation, level_set, labels, contrasts, kernel):
    f32 = jnp.float32
    rows = [x.reshape(128, length) for x in (labels, level_set, perturbation)]
    row_turn = jnp.asarray(twiddles(row_small, row_wide))
    col_turn = twiddles(col_small, col_wide)
    col_turn = jnp.asarray(np.concatenate([col_turn, col_turn], axis=2))
    row_pair, row_first = row_matrices()
    col_pair = column_matrix()

    row_block = pl.BlockSpec((row_step, length), lambda i: (i, 0))
    in_place = pl.BlockSpec(memory_space=pl.ANY)
    scalars = pl.BlockSpec(memory_space=pltpu.SMEM)
    send = pl.pallas_call(
        row_forward,
        in_specs=[scalars] + [in_place] * 6,
        out_shape=jax.ShapeDtypeStruct((length, 128), f32),
        scratch_shapes=[
            pltpu.VMEM((128, length), jnp.int32),
            pltpu.VMEM((128, length), f32),
            pltpu.VMEM((128, length), f32),
            pltpu.VMEM((17, 2, 128), f32),
            pltpu.VMEM((768, 256), bf16),
            pltpu.VMEM((768, 256), bf16),
            pltpu.VMEM((16, 128, 256), f32),
            pltpu.SemaphoreType.DMA((3, steps)),
            pltpu.SemaphoreType.DMA((3,)),
        ],
        compiler_params=params(big),
        cost_estimate=cost(2 * 256 * 768 * 128 * 16, 12 * 2**20),
        name="row_forward",
    )(
        contrasts,
        *rows,
        row_turn,
        jnp.asarray(split_matrix(row_pair.T, 0)),
        jnp.asarray(split_matrix(row_first.T, 0)),
    )

    send, kernel, later = lax.optimization_barrier((send, kernel, rows[:2]))
    received = lax.all_to_all(
        send.reshape(256, 16, 128), ("depth", "rows"), split_axis=0, concat_axis=0, tiled=True
    )
    kernels = pl.pallas_call(
        kernel_in_pairs,
        out_shape=jax.ShapeDtypeStruct((4, 32, 16, 256), f32),
        scratch_shapes=[pltpu.VMEM((length, 128), f32)],
        compiler_params=params(12),
        cost_estimate=cost(2 * 10**9, 4 * 2**20),
        name="kernel_in_pairs",
    )(*exchange_kernel(kernel))

    block = pl.BlockSpec((4, 64, 8, 128), lambda i: (0, 0, i, 0))
    back = pl.pallas_call(
        column,
        grid=(2,),
        in_specs=[
            scalars,
            block,
            pl.BlockSpec((4, 32, 8, 256), lambda i: (0, 0, i, 0)),
            whole((33, 2, 128)),
            whole((768, 256)),
            whole((768, 256)),
        ],
        out_specs=block,
        out_shape=jax.ShapeDtypeStruct((4, 64, 16, 128), f32),
        scratch_shapes=[pltpu.VMEM((4, 34, 8, 256), f32), pltpu.VMEM((32, 8, 128), f32)],
        compiler_params=params(16),
        cost_estimate=cost(2 * 768 * 256 * 4096, 6 * 2**20),
        name="column",
    )(
        lax.axis_index("depth").reshape(1),
        received.reshape(4, 64, 16, 128),
        kernels,
        col_turn,
        jnp.asarray(split_matrix(col_pair.T, 0)),
        jnp.asarray(split_matrix(col_pair, 0)),
    )
    returned = lax.all_to_all(
        back.reshape(256, 16, 128), ("depth", "rows"), split_axis=0, concat_axis=0, tiled=True
    )

    out = pl.pallas_call(
        row_backward,
        grid=(steps,),
        in_specs=[
            scalars,
            row_block,
            row_block,
            whole((length, 128)),
            whole((17, 2, 128)),
            whole((768, 256)),
            whole((768, 256)),
        ],
        out_specs=row_block,
        out_shape=jax.ShapeDtypeStruct((128, length), f32),
        scratch_shapes=[pltpu.VMEM((16, 128, 256), f32)],
        compiler_params=params(16),
        cost_estimate=cost(2 * 256 * 768 * 128 * 16, 6 * 2**20),
        name="row_backward",
    )(
        contrasts,
        *later,
        returned.reshape(length, 128),
        row_turn,
        jnp.asarray(split_matrix(row_pair, 0)),
        jnp.asarray(split_matrix(row_first, 0)),
    )
    return out.reshape(perturbation.shape)


def solution(mesh):
    in_specs = (
        P("depth", "rows", None),
        P("depth", "rows", None),
        P("depth", "rows", None),
        P(),
        P("depth", "rows", None),
    )
    out_specs = P("depth", "rows", None)
    return jax.shard_map(
        on_device, mesh=mesh, in_specs=in_specs, out_specs=out_specs, check_vma=False
    )
```

```python
import math

import jax
import jax.numpy as jnp
import ml_dtypes
import numpy as np
from jax import lax
from jax.experimental import pallas as pl
from jax.experimental.pallas import tpu as pltpu
from jax.sharding import PartitionSpec as P

smoothing = 0.5
length = 4096
big = 60
bf16 = jnp.bfloat16


def cas(angle):
    return np.cos(angle) + np.sin(angle)


def stage_matrices(small, wide):
    b = np.arange(wide)[None, :]
    m = np.arange(wide)[:, None]
    turn = 2.0 * np.pi / wide
    low = np.concatenate([cas(turn * b * m), np.sin(turn * b * m) - np.cos(turn * b * m)], axis=1)
    high = np.concatenate(
        [cas(turn * b * (m + 1)), np.cos(turn * b * (m + 1)) - np.sin(turn * b * (m + 1))], axis=1
    )
    pair = np.concatenate([low, high], axis=0)
    first = np.zeros_like(pair)
    first[:wide, :wide] = cas(turn * b * m)
    full = 2.0 * np.pi / (small * wide)
    first[wide:, wide:] = cas(full * ((b * (small // 2 + small * m)) % (small * wide)))
    scale = 1.0 / math.sqrt(small * wide)
    return pair * scale, first * scale


def twiddles(small, wide):
    k = np.arange(small // 2 + 1)[:, None]
    b = np.arange(wide)[None, :]
    angle = 2.0 * np.pi / (small * wide) * k * b
    return np.stack([np.cos(angle), -np.sin(angle)], axis=1).astype(np.float32)


def split_matrix(matrix, axis):
    high = matrix.astype(ml_dtypes.bfloat16)
    low = (matrix - high.astype(np.float64)).astype(ml_dtypes.bfloat16)
    return np.concatenate([high, high, low], axis=axis)


def split_value(value, axis):
    high = value.astype(bf16)
    low = (value - high.astype(jnp.float32)).astype(bf16)
    return jnp.concatenate([high, low, high], axis=axis)


def dot(a, b, dims):
    return lax.dot_general(a, b, (dims, ((), ())), preferred_element_type=jnp.float32)


def real_fft(values):
    n = len(values)
    if n == 1:
        return [(values[0], None)]
    if n == 2:
        return [(values[0] + values[1], None), (values[0] - values[1], None)]
    even = real_fft(values[0::2])
    odd = real_fft(values[1::2])
    out = [None] * (n // 2 + 1)
    out[0] = (even[0][0] + odd[0][0], None)
    out[n // 2] = (even[0][0] - odd[0][0], None)
    out[n // 4] = (even[n // 4][0], -odd[n // 4][0])
    for k in range(1, n // 4):
        c, s = math.cos(2.0 * math.pi * k / n), math.sin(2.0 * math.pi * k / n)
        er, ei = even[k]
        orr, oi = odd[k]
        if 8 * k == n:
            tr, ti = (orr + oi) * c, (oi - orr) * c
        else:
            tr, ti = orr * c + oi * s, oi * c - orr * s
        out[k] = (er + tr, ei + ti)
        out[n // 2 - k] = (er - tr, ti - ei)
    return out


def real_fft_adjoint(spectrum):
    n = 2 * (len(spectrum) - 1)
    if n == 2:
        return [spectrum[0][0] + spectrum[1][0], spectrum[0][0] - spectrum[1][0]]
    even = [None] * (n // 4 + 1)
    odd = [None] * (n // 4 + 1)
    even[0] = (spectrum[0][0] + spectrum[n // 2][0], None)
    odd[0] = (spectrum[0][0] - spectrum[n // 2][0], None)
    even[n // 4] = (spectrum[n // 4][0], None)
    odd[n // 4] = (-spectrum[n // 4][1], None)
    for k in range(1, n // 4):
        c, s = math.cos(2.0 * math.pi * k / n), math.sin(2.0 * math.pi * k / n)
        ar, ai = spectrum[k]
        br, bi = spectrum[n // 2 - k]
        even[k] = (ar + br, ai - bi)
        dr, di = ar - br, ai + bi
        if 8 * k == n:
            odd[k] = ((dr - di) * c, (dr + di) * c)
        else:
            odd[k] = (dr * c - di * s, dr * s + di * c)
    out = [None] * n
    out[0::2] = real_fft_adjoint(even)
    out[1::2] = real_fft_adjoint(odd)
    return out


row_small, row_wide = 32, 128
col_small, col_wide = 64, 64
row_step = 64
steps = 128 // row_step


def block_rows(k, odd):
    return pl.ds((2 * odd + k // 16) * 64 * 16 + k % 16, 64, stride=16)


def row_forward(contrasts, labels, level_set, perturbation, turn, pair, first, send, *scratch):
    label_buf, level_buf, field_buf, turn_buf, pair_buf, first_buf, parts, block_sem, const_sem = scratch
    copies = []
    for step in range(steps):
        rows = pl.ds(step * row_step, row_step)
        for i, (source, into) in enumerate(
            ((labels, label_buf), (level_set, level_buf), (perturbation, field_buf))
        ):
            copies.append(pltpu.make_async_copy(source.at[rows], into.at[rows], block_sem.at[i, step]))
    constants = [
        pltpu.make_async_copy(source, into, const_sem.at[i])
        for i, (source, into) in enumerate(((turn, turn_buf), (pair, pair_buf), (first, first_buf)))
    ]
    constants[0].start()
    for copy in copies:
        copy.start()
    for copy in constants[1:]:
        copy.start()
    scaled = [contrasts[unit] * (smoothing / math.pi) for unit in range(4)]
    constants[0].wait()
    for step in range(steps):
        for copy in copies[3 * step : 3 * step + 3]:
            copy.wait()

        def tile_of(tile, carry):
            rows = pl.ds(pl.multiple_of(step * row_step + tile * 8, 8), 8)
            fields = []
            for a in range(row_small):
                at = (rows, pl.ds(a * row_wide, row_wide))
                fields.append(unit_weight(scaled, label_buf[at], level_buf[at]) * field_buf[at])
            spectrum = real_fft(fields)
            parts[0, rows, :row_wide] = spectrum[0][0]
            parts[0, rows, row_wide:] = spectrum[row_small // 2][0]
            for k in range(1, row_small // 2):
                re, im = spectrum[k]
                c, s = turn_buf[k, 0:1, :], turn_buf[k, 1:2, :]
                parts[k, rows, :row_wide] = re * c - im * s
                parts[k, rows, row_wide:] = im * c + re * s
            return carry

        lax.fori_loop(0, row_step // 8, tile_of, 0)
    for copy in constants[1:]:
        copy.wait()
    for k in range(row_small // 2):
        value = split_value(parts[k], 1)
        out = dot(value, (pair_buf if k else first_buf)[...], ((1,), (0,))).T
        for half, place in enumerate((k, row_small - k if k else row_small // 2)):
            for odd in range(2):
                begin = (half * 2 + odd) * 64
                send[block_rows(place, odd), :] = out[begin : begin + 64]


def unit_weight(scaled, unit, level):
    chosen = jnp.where(
        unit < 2,
        jnp.where(unit == 0, scaled[0], scaled[1]),
        jnp.where(unit == 2, scaled[2], scaled[3]),
    )
    return chosen / (level * level + smoothing * smoothing)


def row_backward(contrasts, labels, level_set, received, turn, pair, first, out, parts):
    step = pl.program_id(0)
    scaled = [contrasts[unit] * (smoothing / math.pi) for unit in range(4)]

    @pl.when(step == 0)
    def _():
        for k in range(row_small // 2):
            value = jnp.concatenate(
                [
                    received[block_rows(place, odd), :]
                    for place in (k, row_small - k if k else row_small // 2)
                    for odd in range(2)
                ],
                axis=0,
            )
            value = split_value(value, 0)
            matrix = (pair if k else first)[...]
            parts[k] = dot(value, matrix, ((0,), (0,)))

    for tile in range(row_step // 8):
        rows = pl.ds(tile * 8, 8)
        source = pl.ds(pl.multiple_of(step * row_step + tile * 8, 8), 8)
        spectrum = [(parts[0, source, :row_wide], None)]
        for k in range(1, row_small // 2):
            tr, ti = parts[k, source, :row_wide], parts[k, source, row_wide:]
            c, s = turn[k, 0:1, :], turn[k, 1:2, :]
            spectrum.append((tr * c + ti * s, ti * c - tr * s))
        spectrum.append((parts[0, source, row_wide:], None))
        fields = real_fft_adjoint(spectrum)
        for a in range(row_small):
            at = (rows, pl.ds(a * row_wide, row_wide))
            out[at] = fields[a] * unit_weight(scaled, labels[at], level_set[at])


def column(place, received, kernel, turn, matrix, matrix_back, out, parts, data):
    half = col_small // 2
    lanes = (slice(0, 64), slice(64, 128), slice(128, 192), slice(192, 256))
    blank = jnp.zeros((8, 64), jnp.float32)
    parts[:, half + 1] = jnp.zeros((4, 8, 256), jnp.float32)
    for e in range(4):
        source = place[0] ^ e
        spectrum = real_fft([received[source, r] for r in range(col_small)])
        parts[e, 0, :, :128] = spectrum[0][0]
        parts[e, 0, :, 128:] = jnp.zeros((8, 128), jnp.float32)
        parts[e, half, :, :128] = spectrum[half][0] * turn[half, 0:1, :]
        parts[e, half, :, 128:] = spectrum[half][0] * turn[half, 1:2, :]
        for k in range(1, half):
            re, im = spectrum[k]
            c, s = turn[k, 0:1, :], turn[k, 1:2, :]
            parts[e, k, :, :128] = re * c - im * s
            parts[e, k, :, 128:] = im * c + re * s
        value = split_value(parts[e].reshape(-1, 256), 1)
        result = dot(value, matrix[...], ((1,), (0,))).reshape(half + 2, 8, 256)
        zero, last = result[0], result[half]
        first = jnp.concatenate(
            [zero[:, lanes[0]], last[:, lanes[0]], zero[:, lanes[2]], last[:, lanes[2]]], axis=1
        )
        for k in range(half):
            spectra = (result[k] if k else first) * kernel[e, k]
            spectra = spectra[:, :128] + spectra[:, 128:]
            data[k] = spectra if e == 0 else data[k] + spectra
    for e in range(4):
        for k in range(half):
            scaled = jnp.concatenate([data[k], data[k]], axis=1) * kernel[e, k]
            if k:
                parts[e, k] = scaled
            else:
                low, high, low2, high2 = [scaled[:, at] for at in lanes]
                parts[e, 0] = jnp.concatenate([low, blank, low2, blank], axis=1)
                parts[e, half] = jnp.concatenate([high, blank, high2, blank], axis=1)
        value = split_value(parts[e].reshape(-1, 256), 1)
        parts[e] = dot(value, matrix_back[...], ((1,), (0,))).reshape(half + 2, 8, 256)
        spectrum = [(parts[e, 0, :, :128], None)]
        for k in range(1, half + 1):
            tr, ti = parts[e, k, :, :128], parts[e, k, :, 128:]
            c, s = turn[k, 0:1, :], turn[k, 1:2, :]
            spectrum.append((tr * c + ti * s, ti * c - tr * s if k < half else None))
        fields = real_fft_adjoint(spectrum)
        for r in range(col_small):
            out[place[0] ^ e, r] = fields[r]


def whole(shape):
    return pl.BlockSpec(shape, lambda *_: (0,) * len(shape))


def params(mib):
    return pltpu.CompilerParams(vmem_limit_bytes=mib * 1024 * 1024)


def cost(flops, moved):
    return pl.CostEstimate(flops=flops, bytes_accessed=moved, transcendentals=0)


def column_matrix():
    both = np.zeros((2, 2, col_wide, 2, 2, col_wide))
    shaped = stage_matrices(col_small, col_wide)[0].reshape(2, col_wide, 2, col_wide)
    for layer in range(2):
        both[layer, :, :, :, layer, :] = shaped
    return both.reshape(256, 256)


def row_matrices():
    out = []
    for matrix in stage_matrices(row_small, row_wide):
        shaped = matrix.reshape(2, row_wide // 2, 2, 2 * row_wide)
        out.append(shaped.swapaxes(1, 2).reshape(256, 256))
    return out


def kernel_in_pairs(*refs):
    sources, out, turned = refs[:4], refs[4], refs[5]
    for tile in range(length // 128):
        lanes = pl.ds(tile * 128, 128)
        turned[lanes, :] = jnp.concatenate([x[:, lanes] for x in sources], axis=0).T
    for k in range(col_small // 2):
        places = (k, col_small - k if k else col_small // 2)
        pair = jnp.concatenate(
            [turned[pl.ds(place, col_wide, stride=col_small), :] for place in places], axis=0
        ).T
        for e in range(4):
            for layer in range(2):
                begin = e * 32 + layer * 16
                out[e, k, :, layer * 128 : layer * 128 + 128] = pair[begin : begin + 16]


def exchange_kernel(kernel):
    place = lax.axis_index("depth")
    out = []
    for e in range(4):
        block = lax.dynamic_slice_in_dim(kernel, (place ^ e) * 16, 16, axis=1)
        if e:
            block = lax.ppermute(block, "depth", [(d, d ^ e) for d in range(4)])
        out.append(block.reshape(32, length))
    return out


def on_device(perturbation, level_set, labels, contrasts, kernel):
    f32 = jnp.float32
    rows = [x.reshape(128, length) for x in (labels, level_set, perturbation)]
    row_turn = jnp.asarray(twiddles(row_small, row_wide))
    col_turn = twiddles(col_small, col_wide)
    col_turn = jnp.asarray(np.concatenate([col_turn, col_turn], axis=2))
    row_pair, row_first = row_matrices()
    col_pair = column_matrix()

    row_block = pl.BlockSpec((row_step, length), lambda i: (i, 0))
    in_place = pl.BlockSpec(memory_space=pl.ANY)
    scalars = pl.BlockSpec(memory_space=pltpu.SMEM)
    send = pl.pallas_call(
        row_forward,
        in_specs=[scalars] + [in_place] * 6,
        out_shape=jax.ShapeDtypeStruct((length, 128), f32),
        scratch_shapes=[
            pltpu.VMEM((128, length), jnp.int32),
            pltpu.VMEM((128, length), f32),
            pltpu.VMEM((128, length), f32),
            pltpu.VMEM((17, 2, 128), f32),
            pltpu.VMEM((768, 256), bf16),
            pltpu.VMEM((768, 256), bf16),
            pltpu.VMEM((16, 128, 256), f32),
            pltpu.SemaphoreType.DMA((3, steps)),
            pltpu.SemaphoreType.DMA((3,)),
        ],
        compiler_params=params(big),
        cost_estimate=cost(2 * 256 * 768 * 128 * 16, 12 * 2**20),
        name="row_forward",
    )(
        contrasts,
        *rows,
        row_turn,
        jnp.asarray(split_matrix(row_pair.T, 0)),
        jnp.asarray(split_matrix(row_first.T, 0)),
    )

    send, kernel, later = lax.optimization_barrier((send, kernel, rows[:2]))
    received = lax.all_to_all(
        send.reshape(256, 16, 128), ("depth", "rows"), split_axis=0, concat_axis=0, tiled=True
    )
    kernels = pl.pallas_call(
        kernel_in_pairs,
        out_shape=jax.ShapeDtypeStruct((4, 32, 16, 256), f32),
        scratch_shapes=[pltpu.VMEM((length, 128), f32)],
        compiler_params=params(12),
        cost_estimate=cost(2 * 10**9, 4 * 2**20),
        name="kernel_in_pairs",
    )(*exchange_kernel(kernel))

    block = pl.BlockSpec((4, 64, 8, 128), lambda i: (0, 0, i, 0))
    back = pl.pallas_call(
        column,
        grid=(2,),
        in_specs=[
            scalars,
            block,
            pl.BlockSpec((4, 32, 8, 256), lambda i: (0, 0, i, 0)),
            whole((33, 2, 128)),
            whole((768, 256)),
            whole((768, 256)),
        ],
        out_specs=block,
        out_shape=jax.ShapeDtypeStruct((4, 64, 16, 128), f32),
        scratch_shapes=[pltpu.VMEM((4, 34, 8, 256), f32), pltpu.VMEM((32, 8, 128), f32)],
        compiler_params=params(16),
        cost_estimate=cost(2 * 768 * 256 * 4096, 6 * 2**20),
        name="column",
    )(
        lax.axis_index("depth").reshape(1),
        received.reshape(4, 64, 16, 128),
        kernels,
        col_turn,
        jnp.asarray(split_matrix(col_pair.T, 0)),
        jnp.asarray(split_matrix(col_pair, 0)),
    )
    returned = lax.all_to_all(
        back.reshape(256, 16, 128), ("depth", "rows"), split_axis=0, concat_axis=0, tiled=True
    )

    out = pl.pallas_call(
        row_backward,
        grid=(steps,),
        in_specs=[
            scalars,
            row_block,
            row_block,
            whole((length, 128)),
            whole((17, 2, 128)),
            whole((768, 256)),
            whole((768, 256)),
        ],
        out_specs=row_block,
        out_shape=jax.ShapeDtypeStruct((128, length), f32),
        scratch_shapes=[pltpu.VMEM((16, 128, 256), f32)],
        compiler_params=params(16),
        cost_estimate=cost(2 * 256 * 768 * 128 * 16, 6 * 2**20),
        name="row_backward",
    )(
        contrasts,
        *later,
        returned.reshape(length, 128),
        row_turn,
        jnp.asarray(split_matrix(row_pair, 0)),
        jnp.asarray(split_matrix(row_first, 0)),
    )
    return out.reshape(perturbation.shape)


def solution(mesh):
    in_specs = (
        P("depth", "rows", None),
        P("depth", "rows", None),
        P("depth", "rows", None),
        P(),
        P("depth", "rows", None),
    )
    out_specs = P("depth", "rows", None)
    return jax.shard_map(
        on_device, mesh=mesh, in_specs=in_specs, out_specs=out_specs, check_vma=False
    )
```

```python
import math

import jax
import jax.numpy as jnp
import ml_dtypes
import numpy as np
from jax import lax
from jax.experimental import pallas as pl
from jax.experimental.pallas import tpu as pltpu
from jax.sharding import PartitionSpec as P

smoothing = 0.5
length = 4096
big = 60
bf16 = jnp.bfloat16


def cas(angle):
    return np.cos(angle) + np.sin(angle)


def stage_matrices(small, wide):
    b = np.arange(wide)[None, :]
    m = np.arange(wide)[:, None]
    turn = 2.0 * np.pi / wide
    low = np.concatenate([cas(turn * b * m), np.sin(turn * b * m) - np.cos(turn * b * m)], axis=1)
    high = np.concatenate(
        [cas(turn * b * (m + 1)), np.cos(turn * b * (m + 1)) - np.sin(turn * b * (m + 1))], axis=1
    )
    pair = np.concatenate([low, high], axis=0)
    first = np.zeros_like(pair)
    first[:wide, :wide] = cas(turn * b * m)
    full = 2.0 * np.pi / (small * wide)
    first[wide:, wide:] = cas(full * ((b * (small // 2 + small * m)) % (small * wide)))
    scale = 1.0 / math.sqrt(small * wide)
    return pair * scale, first * scale


def twiddles(small, wide):
    k = np.arange(small // 2 + 1)[:, None]
    b = np.arange(wide)[None, :]
    angle = 2.0 * np.pi / (small * wide) * k * b
    return np.stack([np.cos(angle), -np.sin(angle)], axis=1).astype(np.float32)


def split_matrix(matrix, axis):
    high = matrix.astype(ml_dtypes.bfloat16)
    low = (matrix - high.astype(np.float64)).astype(ml_dtypes.bfloat16)
    return np.concatenate([high, high, low], axis=axis)


def split_value(value, axis):
    high = value.astype(bf16)
    low = (value - high.astype(jnp.float32)).astype(bf16)
    return jnp.concatenate([high, low, high], axis=axis)


def dot(a, b, dims):
    return lax.dot_general(a, b, (dims, ((), ())), preferred_element_type=jnp.float32)


def real_fft(values):
    n = len(values)
    if n == 1:
        return [(values[0], None)]
    if n == 2:
        return [(values[0] + values[1], None), (values[0] - values[1], None)]
    even = real_fft(values[0::2])
    odd = real_fft(values[1::2])
    out = [None] * (n // 2 + 1)
    out[0] = (even[0][0] + odd[0][0], None)
    out[n // 2] = (even[0][0] - odd[0][0], None)
    out[n // 4] = (even[n // 4][0], -odd[n // 4][0])
    for k in range(1, n // 4):
        c, s = math.cos(2.0 * math.pi * k / n), math.sin(2.0 * math.pi * k / n)
        er, ei = even[k]
        orr, oi = odd[k]
        if 8 * k == n:
            tr, ti = (orr + oi) * c, (oi - orr) * c
        else:
            tr, ti = orr * c + oi * s, oi * c - orr * s
        out[k] = (er + tr, ei + ti)
        out[n // 2 - k] = (er - tr, ti - ei)
    return out


def real_fft_adjoint(spectrum):
    n = 2 * (len(spectrum) - 1)
    if n == 2:
        return [spectrum[0][0] + spectrum[1][0], spectrum[0][0] - spectrum[1][0]]
    even = [None] * (n // 4 + 1)
    odd = [None] * (n // 4 + 1)
    even[0] = (spectrum[0][0] + spectrum[n // 2][0], None)
    odd[0] = (spectrum[0][0] - spectrum[n // 2][0], None)
    even[n // 4] = (spectrum[n // 4][0], None)
    odd[n // 4] = (-spectrum[n // 4][1], None)
    for k in range(1, n // 4):
        c, s = math.cos(2.0 * math.pi * k / n), math.sin(2.0 * math.pi * k / n)
        ar, ai = spectrum[k]
        br, bi = spectrum[n // 2 - k]
        even[k] = (ar + br, ai - bi)
        dr, di = ar - br, ai + bi
        if 8 * k == n:
            odd[k] = ((dr - di) * c, (dr + di) * c)
        else:
            odd[k] = (dr * c - di * s, dr * s + di * c)
    out = [None] * n
    out[0::2] = real_fft_adjoint(even)
    out[1::2] = real_fft_adjoint(odd)
    return out


row_small, row_wide = 32, 128
col_small, col_wide = 64, 64
row_step = 32
steps = 128 // row_step


def block_rows(k, odd):
    return pl.ds((2 * odd + k // 16) * 64 * 16 + k % 16, 64, stride=16)


def row_forward(contrasts, labels, level_set, perturbation, turn, pair, first, send, *scratch):
    label_buf, level_buf, field_buf, turn_buf, pair_buf, first_buf, parts, block_sem, const_sem = scratch
    copies = []
    for step in range(steps):
        rows = pl.ds(step * row_step, row_step)
        for i, (source, into) in enumerate(
            ((labels, label_buf), (level_set, level_buf), (perturbation, field_buf))
        ):
            copies.append(pltpu.make_async_copy(source.at[rows], into.at[rows], block_sem.at[i, step]))
    constants = [
        pltpu.make_async_copy(source, into, const_sem.at[i])
        for i, (source, into) in enumerate(((turn, turn_buf), (pair, pair_buf), (first, first_buf)))
    ]
    constants[0].start()
    for copy in copies:
        copy.start()
    for copy in constants[1:]:
        copy.start()
    scaled = [contrasts[unit] * (smoothing / math.pi) for unit in range(4)]
    constants[0].wait()
    for step in range(steps):
        for copy in copies[3 * step : 3 * step + 3]:
            copy.wait()

        def tile_of(tile, carry):
            rows = pl.ds(pl.multiple_of(step * row_step + tile * 8, 8), 8)
            fields = []
            for a in range(row_small):
                at = (rows, pl.ds(a * row_wide, row_wide))
                fields.append(unit_weight(scaled, label_buf[at], level_buf[at]) * field_buf[at])
            spectrum = real_fft(fields)
            parts[0, rows, :row_wide] = spectrum[0][0]
            parts[0, rows, row_wide:] = spectrum[row_small // 2][0]
            for k in range(1, row_small // 2):
                re, im = spectrum[k]
                c, s = turn_buf[k, 0:1, :], turn_buf[k, 1:2, :]
                parts[k, rows, :row_wide] = re * c - im * s
                parts[k, rows, row_wide:] = im * c + re * s
            return carry

        lax.fori_loop(0, row_step // 8, tile_of, 0)
    for copy in constants[1:]:
        copy.wait()
    for k in range(row_small // 2):
        value = split_value(parts[k], 1)
        out = dot(value, (pair_buf if k else first_buf)[...], ((1,), (0,))).T
        for half, place in enumerate((k, row_small - k if k else row_small // 2)):
            for odd in range(2):
                begin = (half * 2 + odd) * 64
                send[block_rows(place, odd), :] = out[begin : begin + 64]


def unit_weight(scaled, unit, level):
    chosen = jnp.where(
        unit < 2,
        jnp.where(unit == 0, scaled[0], scaled[1]),
        jnp.where(unit == 2, scaled[2], scaled[3]),
    )
    return chosen / (level * level + smoothing * smoothing)


def row_backward(contrasts, labels, level_set, received, turn, pair, first, out, parts):
    step = pl.program_id(0)
    scaled = [contrasts[unit] * (smoothing / math.pi) for unit in range(4)]

    @pl.when(step == 0)
    def _():
        for k in range(row_small // 2):
            value = jnp.concatenate(
                [
                    received[block_rows(place, odd), :]
                    for place in (k, row_small - k if k else row_small // 2)
                    for odd in range(2)
                ],
                axis=0,
            )
            value = split_value(value, 0)
            matrix = (pair if k else first)[...]
            parts[k] = dot(value, matrix, ((0,), (0,)))

    for tile in range(row_step // 8):
        rows = pl.ds(tile * 8, 8)
        source = pl.ds(pl.multiple_of(step * row_step + tile * 8, 8), 8)
        spectrum = [(parts[0, source, :row_wide], None)]
        for k in range(1, row_small // 2):
            tr, ti = parts[k, source, :row_wide], parts[k, source, row_wide:]
            c, s = turn[k, 0:1, :], turn[k, 1:2, :]
            spectrum.append((tr * c + ti * s, ti * c - tr * s))
        spectrum.append((parts[0, source, row_wide:], None))
        fields = real_fft_adjoint(spectrum)
        for a in range(row_small):
            at = (rows, pl.ds(a * row_wide, row_wide))
            out[at] = fields[a] * unit_weight(scaled, labels[at], level_set[at])


def column(place, received, early, late, turn, matrix, matrix_back, out, parts, data):
    half = col_small // 2
    kernel = (early.at[0], early.at[1], late.at[0], early.at[2])
    lanes = (slice(0, 64), slice(64, 128), slice(128, 192), slice(192, 256))
    blank = jnp.zeros((8, 64), jnp.float32)
    parts[:, half + 1] = jnp.zeros((4, 8, 256), jnp.float32)
    for e in range(4):
        source = place[0] ^ e
        spectrum = real_fft([received[source, r] for r in range(col_small)])
        parts[e, 0, :, :128] = spectrum[0][0]
        parts[e, 0, :, 128:] = jnp.zeros((8, 128), jnp.float32)
        parts[e, half, :, :128] = spectrum[half][0] * turn[half, 0:1, :]
        parts[e, half, :, 128:] = spectrum[half][0] * turn[half, 1:2, :]
        for k in range(1, half):
            re, im = spectrum[k]
            c, s = turn[k, 0:1, :], turn[k, 1:2, :]
            parts[e, k, :, :128] = re * c - im * s
            parts[e, k, :, 128:] = im * c + re * s
        value = split_value(parts[e].reshape(-1, 256), 1)
        result = dot(value, matrix[...], ((1,), (0,))).reshape(half + 2, 8, 256)
        zero, last = result[0], result[half]
        first = jnp.concatenate(
            [zero[:, lanes[0]], last[:, lanes[0]], zero[:, lanes[2]], last[:, lanes[2]]], axis=1
        )
        for k in range(half):
            spectra = (result[k] if k else first) * kernel[e][k]
            spectra = spectra[:, :128] + spectra[:, 128:]
            data[k] = spectra if e == 0 else data[k] + spectra
    for e in range(4):
        for k in range(half):
            scaled = jnp.concatenate([data[k], data[k]], axis=1) * kernel[e][k]
            if k:
                parts[e, k] = scaled
            else:
                low, high, low2, high2 = [scaled[:, at] for at in lanes]
                parts[e, 0] = jnp.concatenate([low, blank, low2, blank], axis=1)
                parts[e, half] = jnp.concatenate([high, blank, high2, blank], axis=1)
        value = split_value(parts[e].reshape(-1, 256), 1)
        parts[e] = dot(value, matrix_back[...], ((1,), (0,))).reshape(half + 2, 8, 256)
        spectrum = [(parts[e, 0, :, :128], None)]
        for k in range(1, half + 1):
            tr, ti = parts[e, k, :, :128], parts[e, k, :, 128:]
            c, s = turn[k, 0:1, :], turn[k, 1:2, :]
            spectrum.append((tr * c + ti * s, ti * c - tr * s if k < half else None))
        fields = real_fft_adjoint(spectrum)
        for r in range(col_small):
            out[place[0] ^ e, r] = fields[r]


def whole(shape):
    return pl.BlockSpec(shape, lambda *_: (0,) * len(shape))


def params(mib):
    return pltpu.CompilerParams(vmem_limit_bytes=mib * 1024 * 1024)


def cost(flops, moved):
    return pl.CostEstimate(flops=flops, bytes_accessed=moved, transcendentals=0)


def column_matrix():
    both = np.zeros((2, 2, col_wide, 2, 2, col_wide))
    shaped = stage_matrices(col_small, col_wide)[0].reshape(2, col_wide, 2, col_wide)
    for layer in range(2):
        both[layer, :, :, :, layer, :] = shaped
    return both.reshape(256, 256)


def row_matrices():
    out = []
    for matrix in stage_matrices(row_small, row_wide):
        shaped = matrix.reshape(2, row_wide // 2, 2, 2 * row_wide)
        out.append(shaped.swapaxes(1, 2).reshape(256, 256))
    return out


def kernel_in_pairs(*refs):
    sources, out, turned = refs[:-2], refs[-2], refs[-1]
    for tile in range(length // 128):
        lanes = pl.ds(tile * 128, 128)
        turned[lanes, :] = jnp.concatenate([x[:, lanes] for x in sources], axis=0).T
    for k in range(col_small // 2):
        places = (k, col_small - k if k else col_small // 2)
        pair = jnp.concatenate(
            [turned[pl.ds(place, col_wide, stride=col_small), :] for place in places], axis=0
        ).T
        for e in range(len(sources)):
            for layer in range(2):
                begin = e * 32 + layer * 16
                out[e, k, :, layer * 128 : layer * 128 + 128] = pair[begin : begin + 16]


def exchange_kernel(kernel):
    place = lax.axis_index("depth")
    out = []
    for e in range(4):
        block = lax.dynamic_slice_in_dim(kernel, (place ^ e) * 16, 16, axis=1)
        if e:
            block = lax.ppermute(block, "depth", [(d, d ^ e) for d in range(4)])
        out.append(block.reshape(32, length))
    return out


def on_device(perturbation, level_set, labels, contrasts, kernel):
    f32 = jnp.float32
    rows = [x.reshape(128, length) for x in (labels, level_set, perturbation)]
    row_turn = jnp.asarray(twiddles(row_small, row_wide))
    col_turn = twiddles(col_small, col_wide)
    col_turn = jnp.asarray(np.concatenate([col_turn, col_turn], axis=2))
    row_pair, row_first = row_matrices()
    col_pair = column_matrix()

    row_block = pl.BlockSpec((row_step, length), lambda i: (i, 0))
    in_place = pl.BlockSpec(memory_space=pl.ANY)
    scalars = pl.BlockSpec(memory_space=pltpu.SMEM)
    send = pl.pallas_call(
        row_forward,
        in_specs=[scalars] + [in_place] * 6,
        out_shape=jax.ShapeDtypeStruct((length, 128), f32),
        scratch_shapes=[
            pltpu.VMEM((128, length), jnp.int32),
            pltpu.VMEM((128, length), f32),
            pltpu.VMEM((128, length), f32),
            pltpu.VMEM((17, 2, 128), f32),
            pltpu.VMEM((768, 256), bf16),
            pltpu.VMEM((768, 256), bf16),
            pltpu.VMEM((16, 128, 256), f32),
            pltpu.SemaphoreType.DMA((3, steps)),
            pltpu.SemaphoreType.DMA((3,)),
        ],
        compiler_params=params(big),
        cost_estimate=cost(2 * 256 * 768 * 128 * 16, 12 * 2**20),
        name="row_forward",
    )(
        contrasts,
        *rows,
        row_turn,
        jnp.asarray(split_matrix(row_pair.T, 0)),
        jnp.asarray(split_matrix(row_first.T, 0)),
    )

    send, kernel, later = lax.optimization_barrier((send, kernel, rows[:2]))
    received = lax.all_to_all(
        send.reshape(256, 16, 128), ("depth", "rows"), split_axis=0, concat_axis=0, tiled=True
    )
    def in_pairs(*sources):
        return pl.pallas_call(
            kernel_in_pairs,
            out_shape=jax.ShapeDtypeStruct((len(sources), 32, 16, 256), f32),
            scratch_shapes=[pltpu.VMEM((length, 32 * len(sources)), f32)],
            compiler_params=params(12),
            cost_estimate=cost(10**9, 2 * 2**20),
            name="kernel_in_pairs",
        )(*sources)

    blocks = exchange_kernel(kernel)
    early, late = in_pairs(blocks[0], blocks[1], blocks[3]), in_pairs(blocks[2])

    block = pl.BlockSpec((4, 64, 8, 128), lambda i: (0, 0, i, 0))
    back = pl.pallas_call(
        column,
        grid=(2,),
        in_specs=[
            scalars,
            block,
            pl.BlockSpec((3, 32, 8, 256), lambda i: (0, 0, i, 0)),
            pl.BlockSpec((1, 32, 8, 256), lambda i: (0, 0, i, 0)),
            whole((33, 2, 128)),
            whole((768, 256)),
            whole((768, 256)),
        ],
        out_specs=block,
        out_shape=jax.ShapeDtypeStruct((4, 64, 16, 128), f32),
        scratch_shapes=[pltpu.VMEM((4, 34, 8, 256), f32), pltpu.VMEM((32, 8, 128), f32)],
        compiler_params=params(16),
        cost_estimate=cost(2 * 768 * 256 * 4096, 6 * 2**20),
        name="column",
    )(
        lax.axis_index("depth").reshape(1),
        received.reshape(4, 64, 16, 128),
        early,
        late,
        col_turn,
        jnp.asarray(split_matrix(col_pair.T, 0)),
        jnp.asarray(split_matrix(col_pair, 0)),
    )
    returned = lax.all_to_all(
        back.reshape(256, 16, 128), ("depth", "rows"), split_axis=0, concat_axis=0, tiled=True
    )

    out = pl.pallas_call(
        row_backward,
        grid=(steps,),
        in_specs=[
            scalars,
            row_block,
            row_block,
            whole((length, 128)),
            whole((17, 2, 128)),
            whole((768, 256)),
            whole((768, 256)),
        ],
        out_specs=row_block,
        out_shape=jax.ShapeDtypeStruct((128, length), f32),
        scratch_shapes=[pltpu.VMEM((16, 128, 256), f32)],
        compiler_params=params(16),
        cost_estimate=cost(2 * 256 * 768 * 128 * 16, 6 * 2**20),
        name="row_backward",
    )(
        contrasts,
        *later,
        returned.reshape(length, 128),
        row_turn,
        jnp.asarray(split_matrix(row_pair, 0)),
        jnp.asarray(split_matrix(row_first, 0)),
    )
    return out.reshape(perturbation.shape)


def solution(mesh):
    in_specs = (
        P("depth", "rows", None),
        P("depth", "rows", None),
        P("depth", "rows", None),
        P(),
        P("depth", "rows", None),
    )
    out_specs = P("depth", "rows", None)
    return jax.shard_map(
        on_device, mesh=mesh, in_specs=in_specs, out_specs=out_specs, check_vma=False
    )
```
